32 devices in a mesh: groups: 2 (over y), seq: 4 (over z), heads: 2 (over x), users: 2 (over core).
Axes of the slice: x: 2, y: 2, z: 4, core: 2. Of those that a mesh axis runs over, the one named last changes fastest.
Arguments:
- queries: bfloat16 [16, 256, 512], P(('groups', 'users'), 'seq', 'heads'), parts along dimension 0, may hold values from -8 to 8
- keys: bfloat16 [16, 8192, 512], P(('groups', 'users'), 'seq', 'heads'), parts along dimension 0, may hold values from -8 to 8
- values: bfloat16 [16, 8192, 512], P(('groups', 'users'), 'seq', 'heads'), parts along dimension 0, may hold values from -16 to 16
- hist_len: int32 [16], P(('groups', 'users')), parts along dimension 0, may hold values from 1 to 8192, as said below
- block_ids: int32 [16, 256, 4, 8], P(('groups', 'users'), None, 'seq'), parts along dimension 0, may hold values from 0 to 15, as said below
- block_count: int32 [16, 256, 4], P(('groups', 'users'), None, 'seq'), parts along dimension 0, may hold values from 0 to 8, as said below
- out_weight: bfloat16 [512, 512], P('heads'), may hold values from -0.75 to 0.75
Outputs:
- joined: bfloat16 [16, 256, 512], P(('groups', 'users'), 'seq', 'heads'), parts along dimension 0
The draws below stay inside these ranges and needn't reach their ends.
There are 2 independent parts, one for each index of `groups`. The reference program is written for one: setup_inputs(seed, part) draws one part's arguments, and reference() takes and returns one part's arrays. A program takes and returns all parts, laid end to end along the dimension named above; an argument that names none is the same for every part. Nothing has to cross between parts.
Inputs may be any that keep to these rules, and one draw needn't show every extreme that they name: `block_ids`: the first block_count entries of a candidate's list for a shard are distinct blocks of that shard holding at least one event of the user's history; the remaining entries are unused. `block_count`: at least 1 on the first shard for every candidate; 0 exactly on shards holding none of the user's history; equal to 8 for some candidate. `hist_len`: some user's history fills all 8192 events.
All inputs are finite; a program needn't handle non-finite values.
Results may differ from the reference program's by a relative error of at most 0.011.
Values may be sent and summed in bfloat16 or wider, within the bound.
A program may use at most 64 MiB of HBM per device.

```python
import jax
import jax.numpy as jnp
from jax import lax

D = 512
HEADS = 8
HD = 64
C = 256
BLOCK = 128
MAXB = 8
EV_DEV = 2048
HIST = 8192
USERS = 8


def history_plan(key):
    key = jax.random.fold_in(key, 100)
    key_full, key_blocks, key_tail, key_count, key_order = jax.random.split(key, 5)
    blocks_dev = EV_DEV // BLOCK
    shards = HIST // EV_DEV
    total_blocks = HIST // BLOCK
    full_user = jax.random.randint(key_full, (), 0, USERS)
    user_range = jnp.arange(USERS)
    used_blocks = jax.random.randint(key_blocks, (USERS,), 1, total_blocks + 1)
    used_blocks = jnp.where(user_range == full_user, total_blocks, used_blocks)
    tail_events = jax.random.randint(key_tail, (USERS,), 1, BLOCK + 1)
    lengths = (used_blocks - 1) * BLOCK + tail_events
    lengths = jnp.where(user_range == full_user, HIST, lengths)
    shard_first = jnp.arange(shards) * blocks_dev
    valid_blocks = jnp.clip(used_blocks[:, None] - shard_first[None, :], 0, blocks_dev)
    ceiling = jnp.maximum(jnp.minimum(valid_blocks, MAXB), 1)
    counts = jax.random.randint(key_count, (USERS, C, shards), 1, ceiling[:, None, :] + 1)
    counts = jnp.where(valid_blocks[:, None, :] > 0, counts, 0)
    forced = (user_range[:, None, None] == full_user) & (jnp.arange(C)[None, :, None] == 0)
    counts = jnp.where(forced, MAXB, counts)
    raw_scores = jax.random.randint(key_order, (USERS, C, shards, blocks_dev), 0, 1 << 20)
    block_range = jnp.arange(blocks_dev)
    ranked = raw_scores * blocks_dev + block_range
    ranked = jnp.where(block_range[None, None, None, :] < valid_blocks[:, None, :, None], ranked, -1 - block_range)
    _, chosen = lax.top_k(ranked, MAXB)
    return (lengths.astype(jnp.int32), chosen.astype(jnp.int32), counts.astype(jnp.int32))


def draw_hist_len(key, part):
    return history_plan(key)[0]


def draw_block_ids(key, part):
    return history_plan(key)[1]


def draw_block_count(key, part):
    return history_plan(key)[2]


def draw_queries(key, part):
    key = jax.random.fold_in(key, 1)
    key_drawn = jax.random.fold_in(key, 0)
    drawn = jnp.clip(jax.random.normal(key_drawn, (USERS, C, HEADS, HD), jnp.float32), -4.0, 4.0)
    return drawn.reshape(USERS, C, HEADS * HD).astype(jnp.bfloat16)


def draw_keys(key, part):
    key = jax.random.fold_in(key, 2)
    drawn = jnp.clip(jax.random.normal(key, (USERS, HIST, HEADS, HD), jnp.float32), -4.0, 4.0)
    return drawn.reshape(USERS, HIST, HEADS * HD).astype(jnp.bfloat16)


def levels(stream_key, shape, pieces, least, high):
    def one(dim, blocks):
        draws = jax.random.uniform(jax.random.fold_in(jax.random.fold_in(stream_key, 6), dim), (blocks,), jnp.float32, least / len(pieces), high / len(pieces))
        return jnp.repeat(jnp.exp(draws), shape[dim] // blocks).reshape((-1,) + (1,) * (len(shape) - dim - 1))

    gain = one(*pieces[0])
    for cut in pieces[1:]:
        gain = gain * one(*cut)
    return gain


def bell_draw(own_key, shape, spread, limit, cuts=(), kind=jnp.bfloat16):
    values = spread * jax.random.normal(own_key, shape, jnp.float32)
    if cuts:
        values = values * levels(own_key, shape, cuts, -0.22, 0.18)
    return jnp.clip(values, -limit, limit).astype(kind)


def setup_inputs(seed: int = 0, part: int = 0) -> dict:
    arg_keys = jax.random.split(jax.random.key(seed), 8)
    part_splits = jax.random.split(jax.random.fold_in(arg_keys[7], part), 8)
    queries = draw_queries(jax.random.fold_in(jax.random.fold_in(arg_keys[7], part), 71), part)
    keys = draw_keys(jax.random.fold_in(jax.random.fold_in(arg_keys[7], part), 71), part)
    values = bell_draw(part_splits[2], (USERS, HIST, HEADS * HD), 4.0, 16.0, ((0, 2), (1, 4), (2, 2)))
    hist_len = draw_hist_len(jax.random.fold_in(jax.random.fold_in(arg_keys[7], part), 71), part)
    block_ids = draw_block_ids(jax.random.fold_in(jax.random.fold_in(arg_keys[7], part), 71), part)
    block_count = draw_block_count(jax.random.fold_in(jax.random.fold_in(arg_keys[7], part), 71), part)
    out_weight = bell_draw(arg_keys[6], (HEADS * HD, D), HD ** -0.5, 0.75, ((0, 2),))
    return dict(queries=queries, keys=keys, values=values, hist_len=hist_len, block_ids=block_ids, block_count=block_count, out_weight=out_weight)


def shard_mask(id_rows, count_rows, length, shard_index):
    blocks = jnp.arange(EV_DEV // BLOCK, dtype=jnp.int32)
    slot_range = jnp.arange(MAXB, dtype=jnp.int32)
    matches = (id_rows[:, :, None] == blocks[None, None, :]) & (slot_range[None, :, None] < count_rows[:, None, None])
    chosen = jnp.any(matches, axis=1)
    event_chosen = jnp.repeat(chosen, BLOCK, axis=1)
    position = shard_index * EV_DEV + jnp.arange(EV_DEV, dtype=jnp.int32)
    return event_chosen & (position < length)[None, :]


def shard_scores(query_user, key_shard):
    score_scale = HD ** -0.5
    return jnp.einsum('chd,ehd->che', query_user.astype(jnp.float32), key_shard.astype(jnp.float32)) * score_scale


def reference(queries, keys, values, hist_len, block_ids, block_count, out_weight):
    shards = HIST // EV_DEV
    query_all = queries.reshape(USERS, C, HEADS, HD)
    key_all = keys.reshape(USERS, shards, EV_DEV, HEADS, HD)
    value_all = values.reshape(USERS, shards, EV_DEV, HEADS, HD)
    id_all = jnp.transpose(block_ids, (0, 2, 1, 3))
    count_all = jnp.transpose(block_count, (0, 2, 1))
    shard_range = jnp.arange(shards, dtype=jnp.int32)

    def one_user(inputs):
        query_user, key_user, value_user, length, id_user, count_user = inputs

        def max_pass(peak_score, slices):
            key_shard, id_shard, count_shard, shard_index = slices
            selected = shard_mask(id_shard, count_shard, length, shard_index)
            scores = jnp.where(selected[:, None, :], shard_scores(query_user, key_shard), -1e30)
            return jnp.maximum(peak_score, jnp.max(scores, axis=2)), None

        start_peak = jnp.full((C, HEADS), -1e30, jnp.float32)
        peak_score, _ = lax.scan(max_pass, start_peak, (key_user, id_user, count_user, shard_range))

        def sum_pass(running, slices):
            weight_sum, weighted = running
            key_shard, value_shard, id_shard, count_shard, shard_index = slices
            selected = shard_mask(id_shard, count_shard, length, shard_index)
            scores = shard_scores(query_user, key_shard)
            weight = jnp.where(selected[:, None, :], jnp.exp(scores - peak_score[:, :, None]), 0.0)
            weight_sum = weight_sum + jnp.sum(weight, axis=2)
            weight_round = lax.optimization_barrier(weight.astype(jnp.bfloat16))
            weighted = weighted + jnp.einsum('che,ehd->chd', weight_round.astype(jnp.float32), value_shard.astype(jnp.float32))
            return (weight_sum, weighted), None

        start = (jnp.zeros((C, HEADS), jnp.float32), jnp.zeros((C, HEADS, HD), jnp.float32))
        (weight_sum, weighted), _ = lax.scan(sum_pass, start, (key_user, value_user, id_user, count_user, shard_range))
        attended = (weighted / weight_sum[:, :, None]).astype(jnp.bfloat16).reshape(C, HEADS * HD)
        return jnp.dot(attended, out_weight, preferred_element_type=jnp.float32).astype(jnp.bfloat16)

    return lax.map(one_user, (query_all, key_all, value_all, hist_len, id_all, count_all))
```

```python
import functools

import jax
import jax.numpy as jnp
from jax import lax
from jax.experimental import pallas as pl
from jax.experimental.pallas import tpu as pltpu
from jax.sharding import PartitionSpec as P

HD = 64
BLOCK = 128


def passed_along(value, axis, steps):
    count = lax.axis_size(axis)
    pairs = [(source, (source + steps) % count) for source in range(count)]
    return lax.ppermute(value, axis, pairs)


def shard_mask(id_rows, count_rows, length, shard_index, events):
    blocks = jnp.arange(events // BLOCK, dtype=jnp.int32)
    slot_range = jnp.arange(id_rows.shape[1], dtype=jnp.int32)
    matches = (id_rows[:, :, None] == blocks[None, None, :]) & (
        slot_range[None, :, None] < count_rows[:, None, None]
    )
    chosen = jnp.any(matches, axis=1)
    event_chosen = jnp.repeat(chosen, BLOCK, axis=1)
    position = shard_index * events + jnp.arange(events, dtype=jnp.int32)
    return event_chosen & (position < length)[None, :]


def combine(first, second):
    peak_score = jnp.maximum(first[0], second[0])
    scale_first = jnp.exp(first[0] - peak_score)
    scale_second = jnp.exp(second[0] - peak_score)
    weight_sum = first[1] * scale_first + second[1] * scale_second
    weighted = first[2] * jnp.repeat(scale_first, HD, axis=-1) + second[2] * jnp.repeat(
        scale_second, HD, axis=-1
    )
    return (peak_score, weight_sum, weighted)


def ring_body(queries, keys, values, hist_len, block_ids, block_count, out_weight):
    user_count = queries.shape[0]
    visit_rows = queries.shape[1]
    feature_width = queries.shape[2]
    local_heads = feature_width // HD
    events = keys.shape[1]
    seq_size = lax.axis_size("seq")
    seq_place = lax.axis_index("seq")
    key_heads = keys.reshape(user_count, events, local_heads, HD)
    value_heads = values.reshape(user_count, events, local_heads, HD)
    ids_here = block_ids[:, :, 0, :]
    counts_here = block_count[:, :, 0]
    score_scale = HD ** (-0.5)

    def local_part(query_block, id_block, count_block):

        def per_user(inputs):
            query_user, key_user, value_user, length, id_rows, count_rows = inputs
            row_count = query_user.shape[0]
            selected = shard_mask(id_rows, count_rows, length, seq_place, events)
            query_split = query_user.reshape(row_count, local_heads, HD)
            scores = (
                jnp.einsum(
                    "rhd,ehd->rhe", query_split, key_user, preferred_element_type=jnp.float32
                )
                * score_scale
            )
            scores = jnp.where(selected[:, None, :], scores, -1e30)
            peak_score = jnp.max(scores, axis=2)
            weight = jnp.where(selected[:, None, :], jnp.exp(scores - peak_score[:, :, None]), 0.0)
            weight_sum = jnp.sum(weight, axis=2)
            weighted = jnp.einsum(
                "rhe,ehd->rhd",
                weight.astype(jnp.bfloat16),
                value_user,
                preferred_element_type=jnp.float32,
            )
            return (peak_score, weight_sum, weighted.reshape(row_count, feature_width))

        return lax.map(
            per_user, (query_block, key_heads, value_heads, hist_len, id_block, count_block)
        )

    def tour_step(step_index, running):
        travel_query, peak_score, weight_sum, weighted = running
        anchor = (seq_place - step_index) % seq_size
        first_row = anchor * visit_rows
        id_block = lax.dynamic_slice_in_dim(ids_here, first_row, visit_rows, 1)
        count_block = lax.dynamic_slice_in_dim(counts_here, first_row, visit_rows, 1)
        partial_value = local_part(travel_query, id_block, count_block)
        peak_score, weight_sum, weighted = combine(
            (peak_score, weight_sum, weighted), partial_value
        )
        travel_query = passed_along(travel_query, "seq", 1)
        peak_score, weight_sum, weighted = passed_along(
            (peak_score, weight_sum, weighted), "seq", 1
        )
        return (travel_query, peak_score, weight_sum, weighted)

    def two_steps(half_index, running):
        running = tour_step(2 * half_index, running)
        return tour_step(2 * half_index + 1, running)

    start = (
        queries,
        jnp.full((user_count, visit_rows, local_heads), -1e30, jnp.float32),
        jnp.zeros((user_count, visit_rows, local_heads), jnp.float32),
        jnp.zeros((user_count, visit_rows, feature_width), jnp.float32),
    )
    _, peak_score, weight_sum, weighted = lax.fori_loop(0, seq_size // 2, two_steps, start)
    attended = (weighted / jnp.repeat(weight_sum, HD, axis=2)).astype(jnp.bfloat16)
    projected = jnp.einsum("urw,wd->urd", attended, out_weight, preferred_element_type=jnp.float32)
    joined = lax.psum_scatter(
        projected.astype(jnp.bfloat16), "heads", scatter_dimension=2, tiled=True
    )
    return joined


LANES = 128
CHUNK = 256
FAR = -32768.0
MESH = pl.DeviceIdType.MESH


def kernel(
    seq_size, head_size, q_ref, k_hbm, v_hbm, id_ref, count_ref, length_ref, w_ref, out_ref,
    q_all, k_buf, v_buf, mask, place, scores, lse_send, lse_recv, lse_turn, o_send, o_recv,
    p_own, p_send, p_recv,
    kv_sem, q_send_sem, q_recv_sem, o_send_sem, o_recv_sem, l_send_sem, l_recv_sem,
    p_send_sem, p_recv_sem,
):
    users, rows, width = q_ref.shape
    cands = q_all.shape[1]
    events = k_buf.shape[1]
    heads = width // HD
    blocks = events // BLOCK
    me = lax.axis_index("seq")
    hx = lax.axis_index("heads")

    def kv_copy(u, which):
        src, dst = ((k_hbm, k_buf), (v_hbm, v_buf))[which]
        return pltpu.make_async_copy(src.at[u], dst.at[u], kv_sem.at[u, which])

    def row_range(s):
        return pl.ds(pl.multiple_of(s * rows, rows), rows)

    def q_copy(u, block, way, own=False):
        target = me + 1 if way == 0 else me - 1
        return pltpu.make_async_remote_copy(
            src_ref=q_ref.at[u] if own else q_all.at[u, row_range(block)],
            dst_ref=q_all.at[u, row_range(block)],
            send_sem=q_send_sem.at[u, way, block],
            recv_sem=q_recv_sem.at[u, block],
            device_id={"seq": target},
            device_id_type=MESH,
        )

    def o_copy(u, j):
        to = lax.rem(me + j, seq_size)
        return pltpu.make_async_remote_copy(
            src_ref=o_send.at[u, row_range(to)],
            dst_ref=o_recv.at[u, me],
            send_sem=o_send_sem.at[u, j],
            recv_sem=o_recv_sem.at[u, j],
            device_id={"seq": to},
            device_id_type=MESH,
        )

    def l_copy(u, j):
        to = lax.rem(me + j, seq_size)
        return pltpu.make_async_remote_copy(
            src_ref=lse_send.at[u],
            dst_ref=lse_recv.at[u, me],
            send_sem=l_send_sem.at[u, j],
            recv_sem=l_recv_sem.at[u, j],
            device_id={"seq": to},
            device_id_type=MESH,
        )

    def p_copy(u, j):
        return pltpu.make_async_remote_copy(
            src_ref=p_send.at[u, j],
            dst_ref=p_recv.at[u, j],
            send_sem=p_send_sem.at[u, j],
            recv_sem=p_recv_sem.at[u, j],
            device_id={"heads": lax.rem(hx + j, head_size)},
            device_id_type=MESH,
        )

    def each_user(step):
        def run(u, carry):
            step(u)
            return carry

        lax.fori_loop(0, users, run, 0)

    @each_user
    def _(u):
        kv_copy(u, 0).start()
        kv_copy(u, 1).start()

    barrier = pltpu.get_barrier_semaphore()
    for j in range(1, seq_size):
        pl.semaphore_signal(
            barrier, inc=1, device_id={"seq": lax.rem(me + j, seq_size)}, device_id_type=MESH
        )
    for j in range(1, head_size):
        pl.semaphore_signal(
            barrier, inc=1, device_id={"heads": lax.rem(hx + j, head_size)}, device_id_type=MESH
        )
    pl.semaphore_wait(barrier, seq_size + head_size - 2)

    @each_user
    def _(u):
        @pl.when(me < seq_size - 1)
        def _():
            q_copy(u, me, 0, own=True).start()

        @pl.when(me > 0)
        def _():
            q_copy(u, me, 1, own=True).start()

    def q_round(u, r):
        @pl.when(me - r >= 0)
        def _():
            q_copy(u, me - r, 0).wait_recv()

            @pl.when(me < seq_size - 1)
            def _():
                q_copy(u, me - r, 0).start()

        @pl.when(me + r < seq_size)
        def _():
            q_copy(u, me + r, 1).wait_recv()

            @pl.when(me > 0)
            def _():
                q_copy(u, me + r, 1).start()

    lane = lax.broadcasted_iota(jnp.int32, (cands, LANES), 1)

    @each_user
    def _(u):
        q_all[u, row_range(me), :] = q_ref[u]
        chosen = jnp.zeros((cands, LANES), jnp.bool_)
        ids = id_ref[u]
        count = count_ref[u]
        for i in range(ids.shape[1]):
            chosen = chosen | ((ids[:, i : i + 1] == lane) & (count > i))
        mask[u] = jnp.where(chosen | (lane > blocks), 0.0, FAR).astype(jnp.bfloat16)

    def placed(u):
        event = lax.broadcasted_iota(jnp.int32, (events, LANES), 0)
        column = lax.broadcasted_iota(jnp.int32, (events, LANES), 1)
        past = me * events + event >= length_ref[u]
        here = (event // BLOCK == column) | ((column == blocks) & past)
        place[...] = jnp.where(here, 1.0, 0.0).astype(jnp.bfloat16)

    for r in range(1, seq_size):
        q_round(0, r)

    def attend(u):
        placed(u)
        kv_copy(u, 0).wait()
        kv_copy(u, 1).wait()
        q_user = q_all[u]
        peak_all = jnp.zeros((cands, LANES), jnp.float32)
        sum_all = jnp.ones((cands, LANES), jnp.float32)
        per_head = -(-(seq_size - 1) // heads)
        outs = []
        for h in range(heads):
            for r in range(1 + h * per_head, min(seq_size, 1 + (h + 1) * per_head)):

                @pl.when(u + 1 < users)
                def _(r=r):
                    q_round(u + 1, r)

            pair = slice(h // 2 * LANES, h // 2 * LANES + LANES)
            half = (lane // HD) == (h % 2)
            q_head = jnp.where(half, q_user[:, pair] * (HD ** -0.5), 0.0).astype(jnp.bfloat16)
            q_wide = jnp.concatenate([q_head, mask[u]], axis=1)
            best = jnp.full((cands, LANES), 2 * FAR, jnp.float32)
            for e in range(0, events, CHUNK):
                k_wide = jnp.concatenate(
                    [k_buf[u, e : e + CHUNK, pair], place[e : e + CHUNK]], axis=1
                )
                part = lax.dot_general(
                    q_wide, k_wide, (((1,), (1,)), ((), ())), preferred_element_type=jnp.float32
                )
                scores[h % 2, :, e : e + CHUNK] = part
                for c in range(0, CHUNK, LANES):
                    best = jnp.maximum(best, part[:, c : c + LANES])
            peak = jnp.max(best, axis=1, keepdims=True)
            total = jnp.zeros((cands, 2 * LANES), jnp.float32)
            for e in range(0, events, CHUNK):
                weight = jnp.exp(scores[h % 2, :, e : e + CHUNK] - peak).astype(jnp.bfloat16)
                v_wide = jnp.concatenate(
                    [v_buf[u, e : e + CHUNK, pair], jnp.ones((CHUNK, LANES), jnp.bfloat16)], axis=1
                )
                total = total + jnp.dot(weight, v_wide, preferred_element_type=jnp.float32)
            weight_sum = total[:, LANES:]
            normal = total[:, :LANES] / weight_sum
            outs.append(normal)
            peak_all = jnp.where(lane == h, peak, peak_all)
            sum_all = jnp.where(lane == h, weight_sum, sum_all)
            if h % 2 == 1:
                joined_pair = jnp.where(lane < HD, outs[h - 1], outs[h]).astype(jnp.bfloat16)
                o_send[u, :, pair] = joined_pair
        lse = peak_all + jnp.log(sum_all)
        lse_send[u] = lse.T[:8]
        lse_recv[u, me] = lse_send[u]
        o_recv[u, me] = o_send[u, row_range(me), :]
        for j in range(1, seq_size):
            o_copy(u, j).start()
            l_copy(u, j).start()

    def combine(u):
        for j in range(1, seq_size):
            o_copy(u, j).wait_recv()
            l_copy(u, j).wait_recv()
        flat = jnp.concatenate([lse_recv[u, s] for s in range(seq_size)], axis=0)
        flat = jnp.pad(flat, ((0, -flat.shape[0] % LANES), (0, 0)))
        lse_turn[...] = flat.T
        mine = lse_turn[row_range(me), :]
        first = lax.broadcasted_iota(jnp.int32, (rows, LANES), 1) < HD
        attended = []
        for h in range(0, heads, 2):
            pair = slice(h // 2 * LANES, h // 2 * LANES + LANES)
            lses = [
                jnp.where(first, mine[:, 8 * s + h : 8 * s + h + 1], mine[:, 8 * s + h + 1 : 8 * s + h + 2])
                for s in range(seq_size)
            ]
            top = functools.reduce(jnp.maximum, lses)
            numer = jnp.zeros((rows, LANES), jnp.float32)
            denom = jnp.zeros((rows, LANES), jnp.float32)
            for s in range(seq_size):
                share = jnp.exp(lses[s] - top)
                numer = numer + share * o_recv[u, s, :, pair].astype(jnp.float32)
                denom = denom + share
            attended.append((numer / denom).astype(jnp.bfloat16))
        attended = jnp.concatenate(attended, axis=1)
        for j in list(range(1, head_size)) + [0]:
            first_column = pl.multiple_of(lax.rem(hx + j, head_size) * width, width)
            part = jnp.dot(
                attended, w_ref[:, pl.ds(first_column, width)], preferred_element_type=jnp.float32
            )
            if j:
                p_send[u, j] = part.astype(jnp.bfloat16)
                p_copy(u, j).start()
            else:
                p_own[u] = part

    def finish(u):
        total = p_own[u]
        for j in range(1, head_size):
            p_copy(u, j).wait_recv()
            total = total + p_recv[u, j].astype(jnp.float32)
        out_ref[u] = total.astype(jnp.bfloat16)

    def stage(t, carry):
        @pl.when(t < users)
        def _():
            attend(t)

        @pl.when((t >= 1) & (t <= users))
        def _():
            combine(t - 1)

        @pl.when(t >= 2)
        def _():
            finish(t - 2)

        return carry

    lax.fori_loop(0, users + 2, stage, 0)

    @each_user
    def _(u):
        for j in range(1, seq_size):
            o_copy(u, j).wait_send()
            l_copy(u, j).wait_send()
        for j in range(1, head_size):
            p_copy(u, j).wait_send()
        for s in range(seq_size):

            @pl.when((me < seq_size - 1) & (s <= me))
            def _(s=s):
                q_copy(u, s, 0).wait_send()

            @pl.when((me > 0) & (s >= me))
            def _(s=s):
                q_copy(u, s, 1).wait_send()


def body(queries, keys, values, hist_len, block_ids, block_count, out_weight):
    users, rows, width = queries.shape
    events = keys.shape[1]
    slots = block_ids.shape[3]
    seq_size = lax.axis_size("seq")
    head_size = lax.axis_size("heads")
    cands = block_ids.shape[1]
    if rows % 16 or width % LANES or events % CHUNK or 8 * seq_size > LANES:
        return ring_body(queries, keys, values, hist_len, block_ids, block_count, out_weight)
    vmem = pl.BlockSpec(memory_space=pltpu.VMEM)
    hbm = pl.BlockSpec(memory_space=pl.ANY)
    bf16, f32 = jnp.bfloat16, jnp.float32
    dma = pltpu.SemaphoreType.DMA
    return pl.pallas_call(
        functools.partial(kernel, seq_size, head_size),
        out_shape=jax.ShapeDtypeStruct(queries.shape, bf16),
        in_specs=[vmem, hbm, hbm, vmem, vmem, pl.BlockSpec(memory_space=pltpu.SMEM), vmem],
        out_specs=vmem,
        scratch_shapes=[
            pltpu.VMEM((users, cands, width), bf16),
            pltpu.VMEM((users, events, width), bf16),
            pltpu.VMEM((users, events, width), bf16),
            pltpu.VMEM((users, cands, LANES), bf16),
            pltpu.VMEM((events, LANES), bf16),
            pltpu.VMEM((2, cands, events), f32),
            pltpu.VMEM((users, 8, cands), f32),
            pltpu.VMEM((users, seq_size, 8, cands), f32),
            pltpu.VMEM((cands, LANES), f32),
            pltpu.VMEM((users, cands, width), bf16),
            pltpu.VMEM((users, seq_size, rows, width), bf16),
            pltpu.VMEM((users, rows, width), f32),
            pltpu.VMEM((users, head_size, rows, width), bf16),
            pltpu.VMEM((users, head_size, rows, width), bf16),
            dma((users, 2)),
            dma((users, 2, seq_size)),
            dma((users, seq_size)),
            dma((users, seq_size)),
            dma((users, seq_size)),
            dma((users, seq_size)),
            dma((users, seq_size)),
            dma((users, head_size)),
            dma((users, head_size)),
        ],
        compiler_params=pltpu.CompilerParams(
            collective_id=0, has_side_effects=True, vmem_limit_bytes=48 * 1024 * 1024
        ),
    )(
        queries, keys, values, block_ids.reshape(users, cands, slots),
        block_count.reshape(users, cands, 1), hist_len, out_weight,
    )


def solution(mesh):
    return jax.shard_map(
        body,
        mesh=mesh,
        in_specs=(
            P(("groups", "users"), "seq", "heads"),
            P(("groups", "users"), "seq", "heads"),
            P(("groups", "users"), "seq", "heads"),
            P(("groups", "users")),
            P(("groups", "users"), None, "seq", None),
            P(("groups", "users"), None, "seq"),
            P("heads", None),
        ),
        out_specs=P(("groups", "users"), "seq", "heads"),
        check_vma=False,
    )
```

```python
import functools

import jax
import jax.numpy as jnp
from jax import lax
from jax.experimental import pallas as pl
from jax.experimental.pallas import tpu as pltpu
from jax.sharding import PartitionSpec as P

HD = 64
BLOCK = 128


def passed_along(value, axis, steps):
    count = lax.axis_size(axis)
    pairs = [(source, (source + steps) % count) for source in range(count)]
    return lax.ppermute(value, axis, pairs)


def shard_mask(id_rows, count_rows, length, shard_index, events):
    blocks = jnp.arange(events // BLOCK, dtype=jnp.int32)
    slot_range = jnp.arange(id_rows.shape[1], dtype=jnp.int32)
    matches = (id_rows[:, :, None] == blocks[None, None, :]) & (
        slot_range[None, :, None] < count_rows[:, None, None]
    )
    chosen = jnp.any(matches, axis=1)
    event_chosen = jnp.repeat(chosen, BLOCK, axis=1)
    position = shard_index * events + jnp.arange(events, dtype=jnp.int32)
    return event_chosen & (position < length)[None, :]


def combine(first, second):
    peak_score = jnp.maximum(first[0], second[0])
    scale_first = jnp.exp(first[0] - peak_score)
    scale_second = jnp.exp(second[0] - peak_score)
    weight_sum = first[1] * scale_first + second[1] * scale_second
    weighted = first[2] * jnp.repeat(scale_first, HD, axis=-1) + second[2] * jnp.repeat(
        scale_second, HD, axis=-1
    )
    return (peak_score, weight_sum, weighted)


def ring_body(queries, keys, values, hist_len, block_ids, block_count, out_weight):
    user_count = queries.shape[0]
    visit_rows = queries.shape[1]
    feature_width = queries.shape[2]
    local_heads = feature_width // HD
    events = keys.shape[1]
    seq_size = lax.axis_size("seq")
    seq_place = lax.axis_index("seq")
    key_heads = keys.reshape(user_count, events, local_heads, HD)
    value_heads = values.reshape(user_count, events, local_heads, HD)
    ids_here = block_ids[:, :, 0, :]
    counts_here = block_count[:, :, 0]
    score_scale = HD ** (-0.5)

    def local_part(query_block, id_block, count_block):

        def per_user(inputs):
            query_user, key_user, value_user, length, id_rows, count_rows = inputs
            row_count = query_user.shape[0]
            selected = shard_mask(id_rows, count_rows, length, seq_place, events)
            query_split = query_user.reshape(row_count, local_heads, HD)
            scores = (
                jnp.einsum(
                    "rhd,ehd->rhe", query_split, key_user, preferred_element_type=jnp.float32
                )
                * score_scale
            )
            scores = jnp.where(selected[:, None, :], scores, -1e30)
            peak_score = jnp.max(scores, axis=2)
            weight = jnp.where(selected[:, None, :], jnp.exp(scores - peak_score[:, :, None]), 0.0)
            weight_sum = jnp.sum(weight, axis=2)
            weighted = jnp.einsum(
                "rhe,ehd->rhd",
                weight.astype(jnp.bfloat16),
                value_user,
                preferred_element_type=jnp.float32,
            )
            return (peak_score, weight_sum, weighted.reshape(row_count, feature_width))

        return lax.map(
            per_user, (query_block, key_heads, value_heads, hist_len, id_block, count_block)
        )

    def tour_step(step_index, running):
        travel_query, peak_score, weight_sum, weighted = running
        anchor = (seq_place - step_index) % seq_size
        first_row = anchor * visit_rows
        id_block = lax.dynamic_slice_in_dim(ids_here, first_row, visit_rows, 1)
        count_block = lax.dynamic_slice_in_dim(counts_here, first_row, visit_rows, 1)
        partial_value = local_part(travel_query, id_block, count_block)
        peak_score, weight_sum, weighted = combine(
            (peak_score, weight_sum, weighted), partial_value
        )
        travel_query = passed_along(travel_query, "seq", 1)
        peak_score, weight_sum, weighted = passed_along(
            (peak_score, weight_sum, weighted), "seq", 1
        )
        return (travel_query, peak_score, weight_sum, weighted)

    def two_steps(half_index, running):
        running = tour_step(2 * half_index, running)
        return tour_step(2 * half_index + 1, running)

    start = (
        queries,
        jnp.full((user_count, visit_rows, local_heads), -1e30, jnp.float32),
        jnp.zeros((user_count, visit_rows, local_heads), jnp.float32),
        jnp.zeros((user_count, visit_rows, feature_width), jnp.float32),
    )
    _, peak_score, weight_sum, weighted = lax.fori_loop(0, seq_size // 2, two_steps, start)
    attended = (weighted / jnp.repeat(weight_sum, HD, axis=2)).astype(jnp.bfloat16)
    projected = jnp.einsum("urw,wd->urd", attended, out_weight, preferred_element_type=jnp.float32)
    joined = lax.psum_scatter(
        projected.astype(jnp.bfloat16), "heads", scatter_dimension=2, tiled=True
    )
    return joined


LANES = 128
CHUNK = 256
FAR = -32768.0
MESH = pl.DeviceIdType.MESH


def kernel(
    seq_size, head_size, q_hbm, k_hbm, v_hbm, id_ref, count_ref, length_ref, w_hbm, out_ref,
    q_all, w_ref, k_buf, v_buf, mask, place, scores, lse_send, lse_recv, lse_turn, o_send, o_recv,
    p_own, p_send, p_recv,
    kv_sem, q_own_sem, w_sem, q_send_sem, q_recv_sem, o_send_sem, o_recv_sem, l_send_sem, l_recv_sem,
    p_send_sem, p_recv_sem,
):
    users, rows, width = q_hbm.shape
    cands = q_all.shape[1]
    events = k_buf.shape[1]
    heads = width // HD
    blocks = events // BLOCK
    me = lax.axis_index("seq")
    hx = lax.axis_index("heads")

    def kv_copy(u, which):
        src, dst = ((k_hbm, k_buf), (v_hbm, v_buf))[which]
        return pltpu.make_async_copy(src.at[u], dst.at[u], kv_sem.at[u, which])

    def row_range(s):
        return pl.ds(pl.multiple_of(s * rows, rows), rows)

    def q_copy(u, j):
        return pltpu.make_async_remote_copy(
            src_ref=q_hbm.at[u],
            dst_ref=q_all.at[u, row_range(me)],
            send_sem=q_send_sem.at[u, j],
            recv_sem=q_recv_sem.at[u, j],
            device_id={"seq": lax.rem(me + j, seq_size)},
            device_id_type=MESH,
        )

    def o_copy(u, j):
        to = lax.rem(me + j, seq_size)
        return pltpu.make_async_remote_copy(
            src_ref=o_send.at[u, row_range(to)],
            dst_ref=o_recv.at[u, me],
            send_sem=o_send_sem.at[u, j],
            recv_sem=o_recv_sem.at[u, j],
            device_id={"seq": to},
            device_id_type=MESH,
        )

    def l_copy(u, j):
        to = lax.rem(me + j, seq_size)
        return pltpu.make_async_remote_copy(
            src_ref=lse_send.at[u, to * rows // LANES],
            dst_ref=lse_recv.at[u, me],
            send_sem=l_send_sem.at[u, j],
            recv_sem=l_recv_sem.at[u, j],
            device_id={"seq": to},
            device_id_type=MESH,
        )

    def q_own(u):
        return pltpu.make_async_copy(q_hbm.at[u], q_all.at[u, row_range(me)], q_own_sem.at[u])

    def p_copy(u, j):
        return pltpu.make_async_remote_copy(
            src_ref=p_send.at[u, j],
            dst_ref=p_recv.at[u, j],
            send_sem=p_send_sem.at[u, j],
            recv_sem=p_recv_sem.at[u, j],
            device_id={"heads": lax.rem(hx + j, head_size)},
            device_id_type=MESH,
        )

    def each_user(step):
        def run(u, carry):
            step(u)
            return carry

        lax.fori_loop(0, users, run, 0)

    @each_user
    def _(u):
        q_own(u).start()
        kv_copy(u, 0).start()
        kv_copy(u, 1).start()

    w_copy = pltpu.make_async_copy(w_hbm, w_ref, w_sem)
    w_copy.start()

    barrier = pltpu.get_barrier_semaphore()
    for j in range(1, seq_size):
        pl.semaphore_signal(
            barrier, inc=1, device_id={"seq": lax.rem(me + j, seq_size)}, device_id_type=MESH
        )
    for j in range(1, head_size):
        pl.semaphore_signal(
            barrier, inc=1, device_id={"heads": lax.rem(hx + j, head_size)}, device_id_type=MESH
        )
    pl.semaphore_wait(barrier, seq_size + head_size - 2)

    @each_user
    def _(u):
        for j in range(1, seq_size):
            q_copy(u, j).start()

    lane = lax.broadcasted_iota(jnp.int32, (cands, LANES), 1)

    def prepare(u):
        block = lax.broadcasted_iota(jnp.int32, (LANES, cands), 0)
        chosen = block > blocks
        for i in range(id_ref.shape[1]):
            chosen = chosen | ((id_ref[u, i : i + 1] == block) & (count_ref[u] > i))
        mask[...] = jnp.where(chosen, 0.0, FAR).T.astype(jnp.bfloat16)
        event = lax.broadcasted_iota(jnp.int32, (events, LANES), 0)
        column = lax.broadcasted_iota(jnp.int32, (events, LANES), 1)
        past = me * events + event >= length_ref[u]
        here = (event // BLOCK == column) | ((column == blocks) & past)
        place[...] = jnp.where(here, 1.0, 0.0).astype(jnp.bfloat16)

    prepare(0)
    def attend(u):
        q_own(u).wait()
        for j in range(1, seq_size):
            q_copy(u, j).wait_recv()
        kv_copy(u, 0).wait()
        kv_copy(u, 1).wait()
        q_user = q_all[u]
        peak_all = jnp.zeros((cands, LANES), jnp.float32)
        sum_all = jnp.ones((cands, LANES), jnp.float32)
        outs = []
        for h in range(heads):
            pair = slice(h // 2 * LANES, h // 2 * LANES + LANES)
            half = (lane // HD) == (h % 2)
            q_head = jnp.where(half, q_user[:, pair] * (HD ** -0.5), 0.0).astype(jnp.bfloat16)
            q_wide = jnp.concatenate([q_head, mask[...]], axis=1)
            best = jnp.full((cands, LANES), 2 * FAR, jnp.float32)
            for e in range(0, events, CHUNK):
                k_wide = jnp.concatenate(
                    [k_buf[u, e : e + CHUNK, pair], place[e : e + CHUNK]], axis=1
                )
                part = lax.dot_general(
                    q_wide, k_wide, (((1,), (1,)), ((), ())), preferred_element_type=jnp.float32
                )
                scores[h % 2, :, e : e + CHUNK] = part
                for c in range(0, CHUNK, LANES):
                    best = jnp.maximum(best, part[:, c : c + LANES])
            peak = jnp.max(best, axis=1, keepdims=True)
            total = jnp.zeros((cands, 2 * LANES), jnp.float32)
            for e in range(0, events, CHUNK):
                weight = jnp.exp(scores[h % 2, :, e : e + CHUNK] - peak).astype(jnp.bfloat16)
                v_wide = jnp.concatenate(
                    [v_buf[u, e : e + CHUNK, pair], jnp.ones((CHUNK, LANES), jnp.bfloat16)], axis=1
                )
                total = total + jnp.dot(weight, v_wide, preferred_element_type=jnp.float32)
            weight_sum = total[:, LANES:]
            normal = total[:, :LANES] / weight_sum
            outs.append(normal)
            peak_all = jnp.where(lane == h, peak, peak_all)
            sum_all = jnp.where(lane == h, weight_sum, sum_all)
            if h % 2 == 1:
                joined_pair = jnp.where(lane < HD, outs[h - 1], outs[h]).astype(jnp.bfloat16)
                o_send[u, :, pair] = joined_pair
        lse = peak_all + jnp.log(sum_all)
        turned = lse.T[:8]
        for c in range(cands // LANES):
            lse_send[u, c] = turned[:, c * LANES : (c + 1) * LANES]
        lse_recv[u, me] = lse_send[u, me * rows // LANES]
        o_recv[u, me] = o_send[u, row_range(me), :]
        for j in range(1, seq_size):
            o_copy(u, j).start()
            l_copy(u, j).start()

        @pl.when(u + 1 < users)
        def _():
            prepare(u + 1)

    def combine(u):
        for j in range(1, seq_size):
            o_copy(u, j).wait_recv()
            l_copy(u, j).wait_recv()
        flat = jnp.concatenate([lse_recv[u, s] for s in range(seq_size)], axis=0)
        flat = jnp.pad(flat, ((0, -flat.shape[0] % LANES), (0, 0)))
        lse_turn[...] = flat.T
        mine = lse_turn[pl.ds(pl.multiple_of(lax.rem(me * rows, LANES), rows), rows), :]
        first = lax.broadcasted_iota(jnp.int32, (rows, LANES), 1) < HD
        attended = []
        for h in range(0, heads, 2):
            pair = slice(h // 2 * LANES, h // 2 * LANES + LANES)
            lses = [
                jnp.where(first, mine[:, 8 * s + h : 8 * s + h + 1], mine[:, 8 * s + h + 1 : 8 * s + h + 2])
                for s in range(seq_size)
            ]
            top = functools.reduce(jnp.maximum, lses)
            numer = jnp.zeros((rows, LANES), jnp.float32)
            denom = jnp.zeros((rows, LANES), jnp.float32)
            for s in range(seq_size):
                share = jnp.exp(lses[s] - top)
                numer = numer + share * o_recv[u, s, :, pair].astype(jnp.float32)
                denom = denom + share
            attended.append((numer / denom).astype(jnp.bfloat16))
        attended = jnp.concatenate(attended, axis=1)
        for j in list(range(1, head_size)) + [0]:
            first_column = pl.multiple_of(lax.rem(hx + j, head_size) * width, width)
            part = jnp.dot(
                attended, w_ref[:, pl.ds(first_column, width)], preferred_element_type=jnp.float32
            )
            if j:
                p_send[u, j] = part.astype(jnp.bfloat16)
                p_copy(u, j).start()
            else:
                p_own[u] = part

    def finish(u):
        total = p_own[u]
        for j in range(1, head_size):
            p_copy(u, j).wait_recv()
            total = total + p_recv[u, j].astype(jnp.float32)
        out_ref[u] = total.astype(jnp.bfloat16)

    w_copy.wait()

    def stage(t, carry):
        @pl.when(t < users)
        def _():
            attend(t)

        @pl.when((t >= 2) & (t <= users + 1))
        def _():
            combine(t - 2)

        @pl.when(t >= 3)
        def _():
            finish(t - 3)

        return carry

    lax.fori_loop(0, users + 3, stage, 0)

    @each_user
    def _(u):
        for j in range(1, seq_size):
            o_copy(u, j).wait_send()
            l_copy(u, j).wait_send()
        for j in range(1, head_size):
            p_copy(u, j).wait_send()
        for j in range(1, seq_size):
            q_copy(u, j).wait_send()


def body(queries, keys, values, hist_len, block_ids, block_count, out_weight):
    users, rows, width = queries.shape
    events = keys.shape[1]
    seq_size = lax.axis_size("seq")
    head_size = lax.axis_size("heads")
    cands = block_ids.shape[1]
    if users < 2 or seq_size < 3 or rows % 16 or LANES % rows or width % LANES or events % CHUNK or 8 * seq_size > LANES:
        return ring_body(queries, keys, values, hist_len, block_ids, block_count, out_weight)
    vmem = pl.BlockSpec(memory_space=pltpu.VMEM)
    hbm = pl.BlockSpec(memory_space=pltpu.HBM)
    bf16, f32 = jnp.bfloat16, jnp.float32
    dma = pltpu.SemaphoreType.DMA
    return pl.pallas_call(
        functools.partial(kernel, seq_size, head_size),
        out_shape=jax.ShapeDtypeStruct(queries.shape, bf16),
        in_specs=[hbm, hbm, hbm, vmem, vmem, pl.BlockSpec(memory_space=pltpu.SMEM), hbm],
        out_specs=vmem,
        scratch_shapes=[
            pltpu.VMEM((users, cands, width), bf16),
            pltpu.VMEM(out_weight.shape, bf16),
            pltpu.VMEM((users, events, width), bf16),
            pltpu.VMEM((users, events, width), bf16),
            pltpu.VMEM((cands, LANES), bf16),
            pltpu.VMEM((events, LANES), bf16),
            pltpu.VMEM((2, cands, events), f32),
            pltpu.VMEM((users, cands // LANES, 8, LANES), f32),
            pltpu.VMEM((users, seq_size, 8, LANES), f32),
            pltpu.VMEM((LANES, LANES), f32),
            pltpu.VMEM((users, cands, width), bf16),
            pltpu.VMEM((users, seq_size, rows, width), bf16),
            pltpu.VMEM((users, rows, width), f32),
            pltpu.VMEM((users, head_size, rows, width), bf16),
            pltpu.VMEM((users, head_size, rows, width), bf16),
            dma((users, 2)),
            dma((users,)),
            dma,
            dma((users, seq_size)),
            dma((users, seq_size)),
            dma((users, seq_size)),
            dma((users, seq_size)),
            dma((users, seq_size)),
            dma((users, seq_size)),
            dma((users, head_size)),
            dma((users, head_size)),
        ],
        compiler_params=pltpu.CompilerParams(
            collective_id=0, has_side_effects=True, vmem_limit_bytes=60 * 1024 * 1024
        ),
    )(
        queries, keys, values, jnp.swapaxes(block_ids[:, :, 0, :], 1, 2),
        jnp.swapaxes(block_count, 1, 2), hist_len, out_weight,
    )


def solution(mesh):
    return jax.shard_map(
        body,
        mesh=mesh,
        in_specs=(
            P(("groups", "users"), "seq", "heads"),
            P(("groups", "users"), "seq", "heads"),
            P(("groups", "users"), "seq", "heads"),
            P(("groups", "users")),
            P(("groups", "users"), None, "seq", None),
            P(("groups", "users"), None, "seq"),
            P("heads", None),
        ),
        out_specs=P(("groups", "users"), "seq", "heads"),
        check_vma=False,
    )
```

```python
import functools

import jax
import jax.numpy as jnp
from jax import lax
from jax.experimental import pallas as pl
from jax.experimental.pallas import tpu as pltpu
from jax.sharding import PartitionSpec as P

HD = 64
BLOCK = 128


def passed_along(value, axis, steps):
    count = lax.axis_size(axis)
    pairs = [(source, (source + steps) % count) for source in range(count)]
    return lax.ppermute(value, axis, pairs)


def shard_mask(id_rows, count_rows, length, shard_index, events):
    blocks = jnp.arange(events // BLOCK, dtype=jnp.int32)
    slot_range = jnp.arange(id_rows.shape[1], dtype=jnp.int32)
    matches = (id_rows[:, :, None] == blocks[None, None, :]) & (
        slot_range[None, :, None] < count_rows[:, None, None]
    )
    chosen = jnp.any(matches, axis=1)
    event_chosen = jnp.repeat(chosen, BLOCK, axis=1)
    position = shard_index * events + jnp.arange(events, dtype=jnp.int32)
    return event_chosen & (position < length)[None, :]


def combine(first, second):
    peak_score = jnp.maximum(first[0], second[0])
    scale_first = jnp.exp(first[0] - peak_score)
    scale_second = jnp.exp(second[0] - peak_score)
    weight_sum = first[1] * scale_first + second[1] * scale_second
    weighted = first[2] * jnp.repeat(scale_first, HD, axis=-1) + second[2] * jnp.repeat(
        scale_second, HD, axis=-1
    )
    return (peak_score, weight_sum, weighted)


def ring_body(queries, keys, values, hist_len, block_ids, block_count, out_weight):
    user_count = queries.shape[0]
    visit_rows = queries.shape[1]
    feature_width = queries.shape[2]
    local_heads = feature_width // HD
    events = keys.shape[1]
    seq_size = lax.axis_size("seq")
    seq_place = lax.axis_index("seq")
    key_heads = keys.reshape(user_count, events, local_heads, HD)
    value_heads = values.reshape(user_count, events, local_heads, HD)
    ids_here = block_ids[:, :, 0, :]
    counts_here = block_count[:, :, 0]
    score_scale = HD ** (-0.5)

    def local_part(query_block, id_block, count_block):

        def per_user(inputs):
            query_user, key_user, value_user, length, id_rows, count_rows = inputs
            row_count = query_user.shape[0]
            selected = shard_mask(id_rows, count_rows, length, seq_place, events)
            query_split = query_user.reshape(row_count, local_heads, HD)
            scores = (
                jnp.einsum(
                    "rhd,ehd->rhe", query_split, key_user, preferred_element_type=jnp.float32
                )
                * score_scale
            )
            scores = jnp.where(selected[:, None, :], scores, -1e30)
            peak_score = jnp.max(scores, axis=2)
            weight = jnp.where(selected[:, None, :], jnp.exp(scores - peak_score[:, :, None]), 0.0)
            weight_sum = jnp.sum(weight, axis=2)
            weighted = jnp.einsum(
                "rhe,ehd->rhd",
                weight.astype(jnp.bfloat16),
                value_user,
                preferred_element_type=jnp.float32,
            )
            return (peak_score, weight_sum, weighted.reshape(row_count, feature_width))

        return lax.map(
            per_user, (query_block, key_heads, value_heads, hist_len, id_block, count_block)
        )

    def tour_step(step_index, running):
        travel_query, peak_score, weight_sum, weighted = running
        anchor = (seq_place - step_index) % seq_size
        first_row = anchor * visit_rows
        id_block = lax.dynamic_slice_in_dim(ids_here, first_row, visit_rows, 1)
        count_block = lax.dynamic_slice_in_dim(counts_here, first_row, visit_rows, 1)
        partial_value = local_part(travel_query, id_block, count_block)
        peak_score, weight_sum, weighted = combine(
            (peak_score, weight_sum, weighted), partial_value
        )
        travel_query = passed_along(travel_query, "seq", 1)
        peak_score, weight_sum, weighted = passed_along(
            (peak_score, weight_sum, weighted), "seq", 1
        )
        return (travel_query, peak_score, weight_sum, weighted)

    def two_steps(half_index, running):
        running = tour_step(2 * half_index, running)
        return tour_step(2 * half_index + 1, running)

    start = (
        queries,
        jnp.full((user_count, visit_rows, local_heads), -1e30, jnp.float32),
        jnp.zeros((user_count, visit_rows, local_heads), jnp.float32),
        jnp.zeros((user_count, visit_rows, feature_width), jnp.float32),
    )
    _, peak_score, weight_sum, weighted = lax.fori_loop(0, seq_size // 2, two_steps, start)
    attended = (weighted / jnp.repeat(weight_sum, HD, axis=2)).astype(jnp.bfloat16)
    projected = jnp.einsum("urw,wd->urd", attended, out_weight, preferred_element_type=jnp.float32)
    joined = lax.psum_scatter(
        projected.astype(jnp.bfloat16), "heads", scatter_dimension=2, tiled=True
    )
    return joined


LANES = 128
CHUNK = 256
FAR = -32768.0
MESH = pl.DeviceIdType.MESH


def kernel(
    seq_size, head_size, q_hbm, k_hbm, v_hbm, id_ref, count_ref, length_ref, w_hbm, out_ref,
    q_all, w_ref, k_buf, v_buf, mask, place, scores, lse_send, lse_recv, lse_turn, o_send, o_recv,
    p_own, p_send, p_recv,
    kv_sem, q_own_sem, w_sem, q_send_sem, q_recv_sem, o_send_sem, o_recv_sem, l_send_sem, l_recv_sem,
    p_send_sem, p_recv_sem,
):
    users, rows, width = q_hbm.shape
    cands = q_all.shape[1]
    events = k_buf.shape[1]
    heads = width // HD
    blocks = events // BLOCK
    me = lax.axis_index("seq")
    hx = lax.axis_index("heads")

    def kv_copy(u, which):
        src, dst = ((k_hbm, k_buf), (v_hbm, v_buf))[which]
        return pltpu.make_async_copy(src.at[u], dst.at[u], kv_sem.at[u, which])

    def row_range(s):
        return pl.ds(pl.multiple_of(s * rows, rows), rows)

    def q_copy(u, j):
        return pltpu.make_async_remote_copy(
            src_ref=q_hbm.at[u],
            dst_ref=q_all.at[u, row_range(me)],
            send_sem=q_send_sem.at[u, j],
            recv_sem=q_recv_sem.at[u, j],
            device_id={"seq": lax.rem(me + j, seq_size)},
            device_id_type=MESH,
        )

    def o_copy(u, j):
        to = lax.rem(me + j, seq_size)
        return pltpu.make_async_remote_copy(
            src_ref=o_send.at[u, row_range(to)],
            dst_ref=o_recv.at[u, me],
            send_sem=o_send_sem.at[u, j],
            recv_sem=o_recv_sem.at[u, j],
            device_id={"seq": to},
            device_id_type=MESH,
        )

    def l_copy(u, j):
        to = lax.rem(me + j, seq_size)
        return pltpu.make_async_remote_copy(
            src_ref=lse_send.at[u, to * rows // LANES],
            dst_ref=lse_recv.at[u, me],
            send_sem=l_send_sem.at[u, j],
            recv_sem=l_recv_sem.at[u, j],
            device_id={"seq": to},
            device_id_type=MESH,
        )

    def q_own(u):
        return pltpu.make_async_copy(q_hbm.at[u], q_all.at[u, row_range(me)], q_own_sem.at[u])

    def p_copy(u, j):
        return pltpu.make_async_remote_copy(
            src_ref=p_send.at[u, j],
            dst_ref=p_recv.at[u, j],
            send_sem=p_send_sem.at[u, j],
            recv_sem=p_recv_sem.at[u, j],
            device_id={"heads": lax.rem(hx + j, head_size)},
            device_id_type=MESH,
        )

    def each_user(step):
        def run(u, carry):
            step(u)
            return carry

        lax.fori_loop(0, users, run, 0)

    @each_user
    def _(u):
        q_own(u).start()
        kv_copy(u, 0).start()
        kv_copy(u, 1).start()

    w_copy = pltpu.make_async_copy(w_hbm, w_ref, w_sem)
    w_copy.start()

    barrier = pltpu.get_barrier_semaphore()
    for j in range(1, seq_size):
        pl.semaphore_signal(
            barrier, inc=1, device_id={"seq": lax.rem(me + j, seq_size)}, device_id_type=MESH
        )
    for j in range(1, head_size):
        pl.semaphore_signal(
            barrier, inc=1, device_id={"heads": lax.rem(hx + j, head_size)}, device_id_type=MESH
        )
    pl.semaphore_wait(barrier, seq_size + head_size - 2)

    @each_user
    def _(u):
        for j in range(1, seq_size):
            q_copy(u, j).start()

    lane = lax.broadcasted_iota(jnp.int32, (cands, LANES), 1)

    def prepare(u):
        block = lax.broadcasted_iota(jnp.int32, (LANES, cands), 0)
        chosen = block > blocks
        for i in range(id_ref.shape[1]):
            chosen = chosen | ((id_ref[u, i : i + 1] == block) & (count_ref[u] > i))
        mask[...] = jnp.where(chosen, 0.0, FAR).T.astype(jnp.bfloat16)
        event = lax.broadcasted_iota(jnp.int32, (events, LANES), 0)
        column = lax.broadcasted_iota(jnp.int32, (events, LANES), 1)
        past = me * events + event >= length_ref[u]
        here = (event // BLOCK == column) | ((column == blocks) & past)
        place[...] = jnp.where(here, 1.0, 0.0).astype(jnp.bfloat16)

    prepare(0)
    def attend(u):
        q_own(u).wait()
        for j in range(1, seq_size):
            q_copy(u, j).wait_recv()
        kv_copy(u, 0).wait()
        kv_copy(u, 1).wait()
        q_user = q_all[u]
        peak_all = jnp.zeros((cands, LANES), jnp.float32)
        sum_all = jnp.ones((cands, LANES), jnp.float32)
        outs = []
        for h in range(heads):
            pair = slice(h // 2 * LANES, h // 2 * LANES + LANES)
            half = (lane // HD) == (h % 2)
            q_head = jnp.where(half, q_user[:, pair] * (HD ** -0.5), 0.0).astype(jnp.bfloat16)
            q_wide = jnp.concatenate([q_head, mask[...]], axis=1)
            best = jnp.full((cands, LANES), 2 * FAR, jnp.float32)
            for e in range(0, events, CHUNK):
                k_wide = jnp.concatenate(
                    [k_buf[u, e : e + CHUNK, pair], place[e : e + CHUNK]], axis=1
                )
                part = lax.dot_general(
                    q_wide, k_wide, (((1,), (1,)), ((), ())), preferred_element_type=jnp.float32
                )
                scores[h % 2, :, e : e + CHUNK] = part
                for c in range(0, CHUNK, LANES):
                    best = jnp.maximum(best, part[:, c : c + LANES])
            peak = jnp.max(best, axis=1, keepdims=True)
            total = jnp.zeros((cands, 2 * LANES), jnp.float32)
            for e in range(0, events, CHUNK):
                weight = jnp.exp(scores[h % 2, :, e : e + CHUNK] - peak).astype(jnp.bfloat16)
                v_wide = jnp.concatenate(
                    [v_buf[u, e : e + CHUNK, pair], jnp.ones((CHUNK, LANES), jnp.bfloat16)], axis=1
                )
                total = total + jnp.dot(weight, v_wide, preferred_element_type=jnp.float32)
            weight_sum = total[:, LANES:]
            normal = total[:, :LANES] / weight_sum
            outs.append(normal)
            peak_all = jnp.where(lane == h, peak, peak_all)
            sum_all = jnp.where(lane == h, weight_sum, sum_all)
            if h % 2 == 1:
                joined_pair = jnp.where(lane < HD, outs[h - 1], outs[h]).astype(jnp.bfloat16)
                o_send[u, :, pair] = joined_pair
        lse = peak_all + jnp.log(sum_all)
        turned = lse.T[:8]
        for c in range(cands // LANES):
            lse_send[u, c] = turned[:, c * LANES : (c + 1) * LANES]
        lse_recv[u, me] = lse_send[u, me * rows // LANES]
        o_recv[u, me] = o_send[u, row_range(me), :]
        for j in range(1, seq_size):
            o_copy(u, j).start()
            l_copy(u, j).start()

        @pl.when(u + 1 < users)
        def _():
            prepare(u + 1)

    def combine(u):
        for j in range(1, seq_size):
            o_copy(u, j).wait_recv()
            l_copy(u, j).wait_recv()
        flat = jnp.concatenate([lse_recv[u, s] for s in range(seq_size)], axis=0)
        flat = jnp.pad(flat, ((0, -flat.shape[0] % LANES), (0, 0)))
        lse_turn[...] = flat.T
        mine = lse_turn[pl.ds(pl.multiple_of(lax.rem(me * rows, LANES), rows), rows), :]
        first = lax.broadcasted_iota(jnp.int32, (rows, LANES), 1) < HD
        attended = []
        for h in range(0, heads, 2):
            pair = slice(h // 2 * LANES, h // 2 * LANES + LANES)
            lses = [
                jnp.where(first, mine[:, 8 * s + h : 8 * s + h + 1], mine[:, 8 * s + h + 1 : 8 * s + h + 2])
                for s in range(seq_size)
            ]
            top = functools.reduce(jnp.maximum, lses)
            numer = jnp.zeros((rows, LANES), jnp.float32)
            denom = jnp.zeros((rows, LANES), jnp.float32)
            for s in range(seq_size):
                share = jnp.exp(lses[s] - top)
                numer = numer + share * o_recv[u, s, :, pair].astype(jnp.float32)
                denom = denom + share
            attended.append((numer / denom).astype(jnp.bfloat16))
        attended = jnp.concatenate(attended, axis=1)
        for j in list(range(1, head_size)) + [0]:
            first_column = pl.multiple_of(lax.rem(hx + j, head_size) * width, width)
            part = jnp.dot(
                attended, w_ref[:, pl.ds(first_column, width)], preferred_element_type=jnp.float32
            )
            if j:
                p_send[u, j] = part.astype(jnp.bfloat16)
                p_copy(u, j).start()
            else:
                p_own[u] = part

    def finish(u):
        total = p_own[u]
        for j in range(1, head_size):
            p_copy(u, j).wait_recv()
            total = total + p_recv[u, j].astype(jnp.float32)
        out_ref[u] = total.astype(jnp.bfloat16)

    w_copy.wait()

    def stage(t, carry):
        @pl.when(t < users)
        def _():
            attend(t)

        @pl.when((t >= 3) & (t < users + 3))
        def _():
            combine(t - 3)

        @pl.when(t >= 4)
        def _():
            finish(t - 4)

        return carry

    lax.fori_loop(0, users + 4, stage, 0)

    @each_user
    def _(u):
        for j in range(1, seq_size):
            o_copy(u, j).wait_send()
            l_copy(u, j).wait_send()
        for j in range(1, head_size):
            p_copy(u, j).wait_send()
        for j in range(1, seq_size):
            q_copy(u, j).wait_send()


def body(queries, keys, values, hist_len, block_ids, block_count, out_weight):
    users, rows, width = queries.shape
    events = keys.shape[1]
    seq_size = lax.axis_size("seq")
    head_size = lax.axis_size("heads")
    cands = block_ids.shape[1]
    if users < 2 or seq_size < 3 or rows % 16 or LANES % rows or width % LANES or events % CHUNK or 8 * seq_size > LANES:
        return ring_body(queries, keys, values, hist_len, block_ids, block_count, out_weight)
    vmem = pl.BlockSpec(memory_space=pltpu.VMEM)
    hbm = pl.BlockSpec(memory_space=pltpu.HBM)
    bf16, f32 = jnp.bfloat16, jnp.float32
    dma = pltpu.SemaphoreType.DMA
    return pl.pallas_call(
        functools.partial(kernel, seq_size, head_size),
        out_shape=jax.ShapeDtypeStruct(queries.shape, bf16),
        in_specs=[hbm, hbm, hbm, vmem, vmem, pl.BlockSpec(memory_space=pltpu.SMEM), hbm],
        out_specs=vmem,
        scratch_shapes=[
            pltpu.VMEM((users, cands, width), bf16),
            pltpu.VMEM(out_weight.shape, bf16),
            pltpu.VMEM((users, events, width), bf16),
            pltpu.VMEM((users, events, width), bf16),
            pltpu.VMEM((cands, LANES), bf16),
            pltpu.VMEM((events, LANES), bf16),
            pltpu.VMEM((2, cands, events), f32),
            pltpu.VMEM((users, cands // LANES, 8, LANES), f32),
            pltpu.VMEM((users, seq_size, 8, LANES), f32),
            pltpu.VMEM((LANES, LANES), f32),
            pltpu.VMEM((users, cands, width), bf16),
            pltpu.VMEM((users, seq_size, rows, width), bf16),
            pltpu.VMEM((users, rows, width), f32),
            pltpu.VMEM((users, head_size, rows, width), bf16),
            pltpu.VMEM((users, head_size, rows, width), bf16),
            dma((users, 2)),
            dma((users,)),
            dma,
            dma((users, seq_size)),
            dma((users, seq_size)),
            dma((users, seq_size)),
            dma((users, seq_size)),
            dma((users, seq_size)),
            dma((users, seq_size)),
            dma((users, head_size)),
            dma((users, head_size)),
        ],
        compiler_params=pltpu.CompilerParams(
            collective_id=0, has_side_effects=True, vmem_limit_bytes=60 * 1024 * 1024
        ),
    )(
        queries, keys, values, jnp.swapaxes(block_ids[:, :, 0, :], 1, 2),
        jnp.swapaxes(block_count, 1, 2), hist_len, out_weight,
    )


def solution(mesh):
    return jax.shard_map(
        body,
        mesh=mesh,
        in_specs=(
            P(("groups", "users"), "seq", "heads"),
            P(("groups", "users"), "seq", "heads"),
            P(("groups", "users"), "seq", "heads"),
            P(("groups", "users")),
            P(("groups", "users"), None, "seq", None),
            P(("groups", "users"), None, "seq"),
            P("heads", None),
        ),
        out_specs=P(("groups", "users"), "seq", "heads"),
        check_vma=False,
    )
```
